32 devices in a mesh: outer: 4 (over y, x), inner: 8 (over z, core).
Axes of the slice: x: 2, y: 2, z: 4, core: 2. Of those that a mesh axis runs over, the one named last changes fastest.
Arguments:
- jacobians: float32 [32, 256, 256], P(('outer', 'inner')), may hold values from -1 to 1, as said below
- weights: float32 [32, 256, 256], P(('outer', 'inner')), may hold values from -3 to 3, as said below
Outputs:
- transitions: float32 [32, 256, 256], P(('outer', 'inner'))
- gramians: float32 [4, 256, 256], P('outer', 'inner')
The draws below stay inside these ranges and needn't reach their ends.
Inputs may be any that keep to these rules, and one draw needn't show every extreme that they name: `jacobians`: each Jacobian's singular values lie within one percent of 1. `weights`: each weight matrix is symmetric.
All inputs are finite; a program needn't handle non-finite values.
Results may differ from the reference program's by a relative error of at most 0.0003.
Values sent between devices are 32-bit elements; how exact they have to be, the bound alone decides.
A program may use at most 64 MiB of HBM per device.

```python
import jax
import jax.numpy as jnp
from jax import lax

S = 256
SEG_STEPS = 8
STEPS = 32
N_OUTER = 4


def orthogonal_like(key):
    base = jax.random.normal(jax.random.fold_in(key, 3), (S, S), jnp.float32)
    start = (jnp.eye(S, dtype=jnp.float32) + 0.6 * base / jnp.sqrt(S * 1.0)) / 1.8
    value = start
    for sweep in range(14):
        value = 1.5 * value - 0.5 * jnp.dot(value, jnp.dot(value.T, value))
    stretch = 1.0 + 0.009 * jax.random.uniform(jax.random.fold_in(key, 5), (S,), jnp.float32, -1.0, 1.0)
    return value * stretch[None, :]


def draw_jacobians(key, part):
    keys = jax.random.split(jax.random.fold_in(key, 11), STEPS)
    return jax.vmap(orthogonal_like)(keys)


def draw_weights(key, part):
    base = jax.random.normal(jax.random.fold_in(key, 23), (STEPS, S, S), jnp.float32)
    sym = 0.25 * (base + jnp.swapaxes(base, 1, 2))
    return jnp.clip(sym, -3.0, 3.0)


def setup_inputs(seed: int = 0) -> dict:
    key_of = jax.random.split(jax.random.key(seed), 3)
    return {
        "jacobians": draw_jacobians(jax.random.fold_in(key_of[2], 71), 0),
        "weights": draw_weights(jax.random.fold_in(key_of[2], 71), 0),
    }


def matmul(left, right):
    return jnp.dot(left, right, precision=lax.Precision.HIGHEST, preferred_element_type=jnp.float32)


def reference(jacobians, weights):
    def advance(carry, pair):
        jac, weight = pair
        current = matmul(jac, carry)
        term = matmul(matmul(current.T, weight), current)
        return current, (current, term)

    start = jnp.eye(S, dtype=jnp.float32)
    _, (transitions, terms) = lax.scan(advance, start, (jacobians, weights))
    gramians = jnp.sum(terms.reshape(N_OUTER, SEG_STEPS, S, S), axis=1)
    return transitions, gramians
```

```python
import functools

import jax
import jax.numpy as jnp
from jax import lax
from jax.experimental import pallas as pl
from jax.experimental.pallas import tpu as pltpu
from jax.sharding import PartitionSpec as P

MESH = pl.DeviceIdType.MESH
CHUNKS = 2


def split(x):
    high = x.astype(jnp.bfloat16)
    return high, (x - high.astype(jnp.float32)).astype(jnp.bfloat16)


def product(left, right, dims=((1,), (0,))):
    dot = functools.partial(
        lax.dot_general, dimension_numbers=(dims, ((), ())), preferred_element_type=jnp.float32
    )
    return dot(left[0], right[0]) + (dot(left[0], right[1]) + dot(left[1], right[0]))


def log2(n):
    return n.bit_length() - 1


def kernel(n_outer, n_inner, jac_hbm, weight_hbm, trans_ref, gram_ref,
           total, other, prefix, weight, term, terms,
           load_sem, send_sem, recv_sem, pass_send, pass_recv, term_send, term_recv):
    outer, inner = lax.axis_index("outer"), lax.axis_index("inner")
    order = prefix.shape[0]
    half = order // 2
    piece = half // CHUNKS
    core = lax.rem(inner, 2)
    sibling = inner + 1 - 2 * core
    load_jac = pltpu.make_async_copy(jac_hbm.at[0], total.at[0], load_sem.at[0])
    load_weight = pltpu.make_async_copy(weight_hbm.at[0], weight, load_sem.at[1])
    load_jac.start()
    load_weight.start()

    def partner(index, bit):
        side = lax.rem(index // (1 << bit), 2)
        return side, index + (1 - 2 * side) * (1 << bit)

    steps = [("inner", b) for b in range(1, log2(n_inner))] + [("outer", b) for b in range(log2(n_outer))]
    barrier = pltpu.get_barrier_semaphore()
    for d in range(1, n_inner):
        pl.semaphore_signal(barrier, inc=1, device_id={"inner": lax.rem(inner + d, n_inner)}, device_id_type=MESH)
    for b in range(log2(n_outer)):
        pl.semaphore_signal(barrier, inc=1, device_id={"outer": partner(outer, b)[1]}, device_id_type=MESH)
    pl.semaphore_wait(barrier, n_inner - 1 + log2(n_outer))

    load_jac.wait()
    swap = pltpu.make_async_remote_copy(
        total.at[0], other.at[0], pass_send.at[0, 0], pass_recv.at[0, 0], {"inner": sibling}, MESH)
    swap.start()
    prefix[...] = total[0]
    swap.wait()
    pending = []

    def exchange(s, side, target, last):
        mine = pl.ds(pl.multiple_of(core * half, half), half)
        theirs = pl.ds(pl.multiple_of((1 - core) * half, half), half)

        @pl.when(side == 1)
        def _():
            right = split(other[s])
            if not last:
                total[s + 1, mine] = product(split(total[s, mine]), right)

        @pl.when(side == 0)
        def _():
            if not last:
                total[s + 1, mine] = product(split(other[s, mine]), split(total[s]))

        copies = []
        if not last:
            for c in range(CHUNKS):
                rows = pl.ds(pl.multiple_of(core * half + c * piece, piece), piece)
                copy = pltpu.make_async_remote_copy(
                    total.at[s + 1, rows], other.at[s + 1, rows],
                    send_sem.at[s + 1, c], recv_sem.at[s + 1, c], target, MESH)
                copy.start()
                copies.append((copy, rows))

        @pl.when(side == 1)
        def _():
            right = split(other[s])
            if not last:
                total[s + 1, theirs] = product(split(total[s, theirs]), right)
            prefix[...] = product(split(prefix[...]), right)

        @pl.when(side == 0)
        def _():
            if not last:
                total[s + 1, theirs] = product(split(other[s, theirs]), split(total[s]))

        passes = []
        for c, (copy, rows) in enumerate(copies):
            copy.wait_recv()
            onward = pltpu.make_async_remote_copy(
                other.at[s + 1, rows], other.at[s + 1, rows],
                pass_send.at[s + 1, c], pass_recv.at[s + 1, c], {"inner": sibling}, MESH)
            onward.start()
            passes.append(onward)
        for onward in passes:
            onward.wait_recv()
        pending.extend(copy for copy, _ in copies)
        pending.extend(passes)

    sides = [core]
    targets = []
    for axis, b in steps:
        side, index = partner(inner if axis == "inner" else outer, b)
        sides.append(side)
        targets.append({axis: index})
    for s in range(len(steps) + 1):
        last = s == len(steps)
        exchange(s, sides[s], None if last else targets[s], last)

    trans_ref[0] = prefix[...]
    current = split(prefix[...])
    load_weight.wait()
    term[...] = product(current, split(product(split(weight[...]), current)), ((0,), (0,)))
    share = order // n_inner
    copies = []
    for d in range(1, n_inner):
        owner = lax.rem(inner + d, n_inner)
        copy = pltpu.make_async_remote_copy(
            term.at[pl.ds(pl.multiple_of(owner * share, share), share)], terms.at[d],
            term_send.at[d], term_recv.at[d], {"inner": owner}, MESH)
        copy.start()
        copies.append(copy)
    result = term[pl.ds(pl.multiple_of(inner * share, share), share)]
    for d in range(1, n_inner):
        copies[d - 1].wait_recv()
        result = result + terms[d]
    gram_ref[0] = result
    for copy in copies + pending:
        copy.wait_send()


def shards(n_outer, n_inner, jacobians, weights):
    order = jacobians.shape[1]
    share = order // n_inner
    levels = log2(n_inner) + log2(n_outer)
    square = (order, order)
    f32 = jnp.float32
    dma = pltpu.SemaphoreType.DMA
    return pl.pallas_call(
        functools.partial(kernel, n_outer, n_inner),
        out_shape=(jax.ShapeDtypeStruct((1,) + square, f32), jax.ShapeDtypeStruct((1, share, order), f32)),
        in_specs=[pl.BlockSpec(memory_space=pl.ANY)] * 2,
        out_specs=[pl.BlockSpec(memory_space=pltpu.VMEM)] * 2,
        scratch_shapes=[
            pltpu.VMEM((levels,) + square, f32),
            pltpu.VMEM((levels,) + square, f32),
            pltpu.VMEM(square, f32),
            pltpu.VMEM(square, f32),
            pltpu.VMEM(square, f32),
            pltpu.VMEM((n_inner, share, order), f32),
            dma((2,)),
            dma((levels, CHUNKS)),
            dma((levels, CHUNKS)),
            dma((levels, CHUNKS)),
            dma((levels, CHUNKS)),
            dma((n_inner,)),
            dma((n_inner,)),
        ],
        compiler_params=pltpu.CompilerParams(
            collective_id=0, has_side_effects=True, vmem_limit_bytes=32 * 1024 * 1024),
    )(jacobians, weights)


def solution(mesh):
    return jax.shard_map(
        functools.partial(shards, mesh.shape["outer"], mesh.shape["inner"]),
        mesh=mesh,
        in_specs=(P(("outer", "inner"), None, None), P(("outer", "inner"), None, None)),
        out_specs=(P(("outer", "inner"), None, None), P("outer", "inner", None)),
        check_vma=False,
    )
```

```python
import functools

import jax
import jax.numpy as jnp
from jax import lax
from jax.experimental import pallas as pl
from jax.experimental.pallas import tpu as pltpu
from jax.sharding import PartitionSpec as P

MESH = pl.DeviceIdType.MESH


def split(x):
    high = x.astype(jnp.bfloat16)
    return high, (x - high.astype(jnp.float32)).astype(jnp.bfloat16)


def product(left, right, dims=((1,), (0,))):
    dot = functools.partial(
        lax.dot_general, dimension_numbers=(dims, ((), ())), preferred_element_type=jnp.float32
    )
    return dot(left[0], right[0]) + (dot(left[0], right[1]) + dot(left[1], right[0]))


def log2(n):
    return n.bit_length() - 1


def kernel(n_outer, n_inner, jac_hbm, weight_hbm, trans_ref, gram_ref,
           total, other, prefix, weight, term, terms, summed, starts, start,
           load_sem, send_sem, recv_sem, pass_send, pass_recv, term_send, term_recv, sum_send, sum_recv,
           start_send, start_recv, start_pass_send, start_pass_recv):
    outer, inner = lax.axis_index("outer"), lax.axis_index("inner")
    order = prefix.shape[0]
    half = order // 2
    core = lax.rem(inner, 2)
    sibling = inner + 1 - 2 * core
    load_jac = pltpu.make_async_copy(jac_hbm.at[0], total.at[0], load_sem.at[0])
    load_weight = pltpu.make_async_copy(weight_hbm.at[0], weight, load_sem.at[1])
    load_jac.start()
    load_weight.start()

    def partner(index, bit):
        side = lax.rem(index // (1 << bit), 2)
        return side, index + (1 - 2 * side) * (1 << bit)

    steps = [("inner", b) for b in range(1, log2(n_inner))]
    barrier = pltpu.get_barrier_semaphore()
    for d in range(1, n_inner):
        pl.semaphore_signal(barrier, inc=1, device_id={"inner": lax.rem(inner + d, n_inner)}, device_id_type=MESH)
    for d in range(1, n_outer):
        pl.semaphore_signal(barrier, inc=1, device_id={"outer": lax.rem(outer + d, n_outer)}, device_id_type=MESH)
    pl.semaphore_wait(barrier, n_inner + n_outer - 2)

    load_jac.wait()
    swap = pltpu.make_async_remote_copy(
        total.at[0], other.at[0], pass_send.at[0], pass_recv.at[0], {"inner": sibling}, MESH)
    swap.start()
    prefix[...] = total[0]
    swap.wait()
    pending = []

    mine = pl.ds(pl.multiple_of(core * half, half), half)
    theirs = pl.ds(pl.multiple_of((1 - core) * half, half), half)
    share = order // n_inner

    def to_segment(d):
        return pltpu.make_async_remote_copy(
            total.at[len(steps) + 1, mine], starts.at[d, mine], start_send.at[d], start_recv.at[d],
            {"outer": lax.rem(outer + d, n_outer)}, MESH)

    def to_sibling(d):
        return pltpu.make_async_remote_copy(
            starts.at[d, mine], starts.at[d, mine], start_pass_send.at[d], start_pass_recv.at[d],
            {"inner": sibling}, MESH)

    def to_owner(d):
        owner = lax.rem(inner + d, n_inner)
        return pltpu.make_async_remote_copy(
            term.at[pl.ds(pl.multiple_of(owner * share, share), share)], terms.at[d],
            term_send.at[d], term_recv.at[d], {"inner": owner}, MESH)

    own = pl.ds(pl.multiple_of(inner * share, share), share)

    def to_all(d):
        return pltpu.make_async_remote_copy(
            summed.at[own], summed.at[own], sum_send.at[d], sum_recv.at[d],
            {"inner": lax.rem(inner + d, n_inner)}, MESH)

    sides = [core] + [partner(inner, b)[0] for _, b in steps]
    targets = [{axis: partner(inner, b)[1]} for axis, b in steps]
    for s in range(len(steps) + 1):
        side, last = sides[s], s == len(steps)

        @pl.when(side == 1)
        def _():
            total[s + 1, mine] = product(split(total[s, mine]), split(other[s]))

        @pl.when(side == 0)
        def _():
            total[s + 1, mine] = product(split(other[s, mine]), split(total[s]))

        if last:
            for d in range(1, n_outer):
                @pl.when(outer + d < n_outer)
                def _(d=d):
                    to_segment(d).start()
        else:
            copy = pltpu.make_async_remote_copy(
                total.at[s + 1, mine], other.at[s + 1, mine], send_sem.at[s + 1], recv_sem.at[s + 1],
                targets[s], MESH)
            copy.start()

        @pl.when(side == 1)
        def _():
            right = split(other[s])
            if not last:
                total[s + 1, theirs] = product(split(total[s, theirs]), right)
            prefix[...] = product(split(prefix[...]), right)

        if not last:
            @pl.when(side == 0)
            def _():
                total[s + 1, theirs] = product(split(other[s, theirs]), split(total[s]))

            copy.wait_recv()
            onward = pltpu.make_async_remote_copy(
                other.at[s + 1, mine], other.at[s + 1, mine], pass_send.at[s + 1], pass_recv.at[s + 1],
                {"inner": sibling}, MESH)
            onward.start()
            onward.wait_recv()
            pending.extend((copy, onward))

    current = split(prefix[...])
    load_weight.wait()
    term[...] = product(current, split(product(split(weight[...]), current)), ((0,), (0,)))
    owners = [to_owner(d) for d in range(1, n_inner)]
    for copy in owners:
        copy.start()
    for d in range(1, n_outer):
        @pl.when(outer >= d)
        def _(d=d):
            to_segment(d).wait_recv()
            to_sibling(d).start()
    result = term[own]
    for d in range(1, n_inner):
        owners[d - 1].wait_recv()
        result = result + terms[d]
    summed[own] = result
    everyone = [to_all(d) for d in range(1, n_inner)]
    for copy in everyone:
        copy.start()

    for d in range(1, n_outer):
        @pl.when(outer >= d)
        def _(d=d):
            to_sibling(d).wait_recv()
            if d == 1:
                start[...] = starts[d]
            else:
                start[...] = product(split(start[...]), split(starts[d]))

    @pl.when(outer == 0)
    def _():
        trans_ref[0] = prefix[...]

    @pl.when(outer > 0)
    def _():
        trans_ref[0] = product(split(prefix[...]), split(start[...]))

    for copy in everyone:
        copy.wait_recv()
    for copy in owners:
        copy.wait_send()

    @pl.when(outer == 0)
    def _():
        gram_ref[0] = summed[own]

    @pl.when(outer > 0)
    def _():
        first = split(start[...])
        term[...] = product(first, split(product(split(summed[...]), first)), ((0,), (0,)))
        gram_ref[0] = term[own]

    for copy in pending + everyone:
        copy.wait_send()
    for d in range(1, n_outer):
        @pl.when(outer + d < n_outer)
        def _(d=d):
            to_segment(d).wait_send()

        @pl.when(outer >= d)
        def _(d=d):
            to_sibling(d).wait_send()


def shards(n_outer, n_inner, jacobians, weights):
    order = jacobians.shape[1]
    share = order // n_inner
    levels = log2(n_inner)
    square = (order, order)
    f32 = jnp.float32
    dma = pltpu.SemaphoreType.DMA
    return pl.pallas_call(
        functools.partial(kernel, n_outer, n_inner),
        out_shape=(jax.ShapeDtypeStruct((1,) + square, f32), jax.ShapeDtypeStruct((1, share, order), f32)),
        in_specs=[pl.BlockSpec(memory_space=pl.ANY)] * 2,
        out_specs=[pl.BlockSpec(memory_space=pltpu.VMEM)] * 2,
        scratch_shapes=[
            pltpu.VMEM((levels + 1,) + square, f32),
            pltpu.VMEM((levels,) + square, f32),
            pltpu.VMEM(square, f32),
            pltpu.VMEM(square, f32),
            pltpu.VMEM(square, f32),
            pltpu.VMEM((n_inner, share, order), f32),
            pltpu.VMEM(square, f32),
            pltpu.VMEM((n_outer,) + square, f32),
            pltpu.VMEM(square, f32),
            dma((2,)),
            dma((levels,)),
            dma((levels,)),
            dma((levels,)),
            dma((levels,)),
            dma((n_inner,)),
            dma((n_inner,)),
            dma((n_inner,)),
            dma((n_inner,)),
            dma((n_outer,)),
            dma((n_outer,)),
            dma((n_outer,)),
            dma((n_outer,)),
        ],
        compiler_params=pltpu.CompilerParams(
            collective_id=0, has_side_effects=True, vmem_limit_bytes=56 * 1024 * 1024),
    )(jacobians, weights)


def solution(mesh):
    return jax.shard_map(
        functools.partial(shards, mesh.shape["outer"], mesh.shape["inner"]),
        mesh=mesh,
        in_specs=(P(("outer", "inner"), None, None), P(("outer", "inner"), None, None)),
        out_specs=(P(("outer", "inner"), None, None), P("outer", "inner", None)),
        check_vma=False,
    )
```

```python
import functools

import jax
import jax.numpy as jnp
from jax import lax
from jax.experimental import pallas as pl
from jax.experimental.pallas import tpu as pltpu
from jax.sharding import PartitionSpec as P

MESH = pl.DeviceIdType.MESH


def split(x):
    high = x.astype(jnp.bfloat16)
    return high, (x - high.astype(jnp.float32)).astype(jnp.bfloat16)


def product(left, right, dims=((1,), (0,))):
    dot = functools.partial(
        lax.dot_general, dimension_numbers=(dims, ((), ())), preferred_element_type=jnp.float32
    )
    return dot(left[0], right[0]) + (dot(left[0], right[1]) + dot(left[1], right[0]))


def log2(n):
    return n.bit_length() - 1


def kernel(n_outer, n_inner, jac_hbm, weight_hbm, trans_ref, gram_ref,
           total, other, prefix, weight, term, terms, joined, summed, starts, start,
           load_sem, send_sem, recv_sem, pass_send, pass_recv, term_send, term_recv, sum_send, sum_recv,
           sum_pass_send, sum_pass_recv,
           start_send, start_recv, start_pass_send, start_pass_recv):
    outer, inner = lax.axis_index("outer"), lax.axis_index("inner")
    order = prefix.shape[0]
    half = order // 2
    core = lax.rem(inner, 2)
    sibling = inner + 1 - 2 * core
    load_jac = pltpu.make_async_copy(jac_hbm.at[0], total.at[0], load_sem.at[0])
    load_weight = pltpu.make_async_copy(weight_hbm.at[0], weight, load_sem.at[1])
    load_jac.start()
    load_weight.start()

    def partner(index, bit):
        side = lax.rem(index // (1 << bit), 2)
        return side, index + (1 - 2 * side) * (1 << bit)

    steps = [("inner", b) for b in range(1, log2(n_inner))]
    barrier = pltpu.get_barrier_semaphore()
    for d in range(1, n_inner):
        pl.semaphore_signal(barrier, inc=1, device_id={"inner": lax.rem(inner + d, n_inner)}, device_id_type=MESH)
    for d in range(1, n_outer):
        pl.semaphore_signal(barrier, inc=1, device_id={"outer": lax.rem(outer + d, n_outer)}, device_id_type=MESH)
    pl.semaphore_wait(barrier, n_inner + n_outer - 2)

    load_jac.wait()
    swap = pltpu.make_async_remote_copy(
        total.at[0], other.at[0], pass_send.at[0], pass_recv.at[0], {"inner": sibling}, MESH)
    swap.start()
    prefix[...] = total[0]
    swap.wait()

    mine = pl.ds(pl.multiple_of(core * half, half), half)
    theirs = pl.ds(pl.multiple_of((1 - core) * half, half), half)
    share = order // n_inner

    def to_segment(d):
        return pltpu.make_async_remote_copy(
            total.at[len(steps) + 1, mine], starts.at[d, mine], start_send.at[d], start_recv.at[d],
            {"outer": lax.rem(outer + d, n_outer)}, MESH)

    def to_sibling(d):
        return pltpu.make_async_remote_copy(
            starts.at[d, mine], starts.at[d, mine], start_pass_send.at[d], start_pass_recv.at[d],
            {"inner": sibling}, MESH)

    chips = n_inner // 2
    piece = half // chips
    own = pl.ds(pl.multiple_of(inner * share, share), share)

    def rows_of(chip):
        return pl.ds(pl.multiple_of(core * half + chip * piece, piece), piece)

    def chip_at(d):
        return lax.rem(inner // 2 + d, chips)

    def to_owner(d):
        return pltpu.make_async_remote_copy(
            term.at[rows_of(chip_at(d))], terms.at[d], term_send.at[d], term_recv.at[d],
            {"inner": chip_at(d) * 2 + core}, MESH)

    kept = rows_of(chip_at(0))

    def to_all(d):
        return pltpu.make_async_remote_copy(
            summed.at[kept], summed.at[kept], sum_send.at[d], sum_recv.at[d],
            {"inner": chip_at(d) * 2 + core}, MESH)

    def sum_to_sibling(d):
        rows = rows_of(chip_at(chips - d))
        return pltpu.make_async_remote_copy(
            summed.at[rows], summed.at[rows], sum_pass_send.at[d], sum_pass_recv.at[d],
            {"inner": sibling}, MESH)

    sides = [core] + [partner(inner, b)[0] for _, b in steps]
    targets = [{axis: partner(inner, b)[1]} for axis, b in steps]
    left_columns = pl.ds(pl.multiple_of(core * half, half), half)
    right_columns = pl.ds(pl.multiple_of((1 - core) * half, half), half)

    def hop(source, target, s, by_row, device, send, recv):
        part = (s, mine) if by_row else (s, slice(None), left_columns)
        return pltpu.make_async_remote_copy(
            source.at[part], target.at[part], send.at[s], recv.at[s], device, MESH)

    def on_kind(kind, act):
        @pl.when(kind == 0)
        def _():
            act(True)

        @pl.when(kind == 1)
        def _():
            act(False)

    def send_half(s, kind):
        on_kind(kind, lambda by_row: hop(total, other, s, by_row, targets[s - 1], send_sem, recv_sem).start())

    def pass_half(s, kind):
        def act(by_row):
            hop(total, other, s, by_row, targets[s - 1], send_sem, recv_sem).wait_recv()
            hop(other, other, s, by_row, {"inner": sibling}, pass_send, pass_recv).start()
        on_kind(kind, act)

    def wait_pass(s, kind):
        on_kind(kind, lambda by_row: hop(
            other, other, s, by_row, {"inner": sibling}, pass_send, pass_recv).wait_recv())

    def join_rows(s, side, rows):
        @pl.when(side == 1)
        def _():
            total[s + 1, rows] = product(split(total[s, rows]), split(other[s]))

        @pl.when(side == 0)
        def _():
            total[s + 1, rows] = product(split(other[s, rows]), split(total[s]))

    def join_early(side, mine, columns):
        @pl.when(side == 1)
        def _():
            total[2, :, columns] = product(split(total[1]), split(other[1, :, columns]))

        @pl.when(side == 0)
        def _():
            total[2, mine] = product(split(other[1, mine]), split(total[1]))

    kinds = [None, sides[1] if len(sides) > 1 else None]
    for s in range(2, len(sides)):
        kinds.append(sides[1] * 1 if s == 2 else inner * 0)
    def sent(s):
        return 1 - kinds[s] if s == 1 else kinds[s]

    for s in range(len(steps) + 1):
        side, last = sides[s], s == len(steps)
        early = s == 1 and not last
        if early:
            join_early(side, mine, left_columns)
        elif s == 0 and not last:
            join_rows(s, side, mine)
            join_rows(s, side, theirs)
        else:
            join_rows(s, side, mine)

        if last:
            for d in range(1, n_outer):
                @pl.when(outer + d < n_outer)
                def _(d=d):
                    to_segment(d).start()
        else:
            send_half(s + 1, sent(s + 1))

        if early:
            wait_pass(s, kinds[s])
            join_early(side, theirs, right_columns)
        elif not last and s > 0:
            join_rows(s, side, theirs)

        @pl.when(side == 1)
        def _():
            prefix[...] = product(split(prefix[...]), split(other[s]))

        if not last:
            pass_half(s + 1, kinds[s + 1])
            if s + 1 != 1 or s + 1 == len(steps):
                wait_pass(s + 1, kinds[s + 1])

    current = split(prefix[...])
    load_weight.wait()
    term[...] = product(current, split(product(split(weight[...]), current)), ((0,), (0,)))
    join = pltpu.make_async_remote_copy(
        term.at[theirs], joined, term_send.at[0], term_recv.at[0], {"inner": sibling}, MESH)
    join.start()
    join.wait_recv()
    term[mine] = term[mine] + joined[...]
    owners = [to_owner(d) for d in range(1, chips)]
    for copy in owners:
        copy.start()
    result = term[kept]
    for d in range(1, chips):
        owners[d - 1].wait_recv()
        result = result + terms[d]
    summed[kept] = result
    everyone = [to_all(d) for d in range(1, chips)]
    for copy in everyone:
        copy.start()
    onward = [sum_to_sibling(d) for d in range(chips)]
    onward[0].start()
    for d in range(1, n_outer):
        @pl.when(outer >= d)
        def _(d=d):
            to_segment(d).wait_recv()
            to_sibling(d).start()
    for d in range(1, chips):
        everyone[d - 1].wait_recv()
        onward[d].start()

    for d in range(1, n_outer):
        @pl.when(outer >= d)
        def _(d=d):
            to_sibling(d).wait_recv()
            if d == 1:
                start[...] = starts[d]
            else:
                start[...] = product(split(start[...]), split(starts[d]))

    @pl.when(outer == 0)
    def _():
        trans_ref[0] = prefix[...]

    @pl.when(outer > 0)
    def _():
        trans_ref[0] = product(split(prefix[...]), split(start[...]))

    for copy in onward:
        copy.wait_recv()
    for copy in owners + [join]:
        copy.wait_send()

    @pl.when(outer == 0)
    def _():
        gram_ref[0] = summed[own]

    @pl.when(outer > 0)
    def _():
        first = split(start[...])
        term[...] = product(first, split(product(split(summed[...]), first)), ((0,), (0,)))
        gram_ref[0] = term[own]

    for copy in everyone + onward:
        copy.wait_send()

    def finish(s):
        on_kind(sent(s), lambda by_row: hop(
            total, other, s, by_row, targets[s - 1], send_sem, recv_sem).wait_send())
        on_kind(kinds[s], lambda by_row: hop(
            other, other, s, by_row, {"inner": sibling}, pass_send, pass_recv).wait_send())

    for s in range(1, len(sides)):
        finish(s)
    for d in range(1, n_outer):
        @pl.when(outer + d < n_outer)
        def _(d=d):
            to_segment(d).wait_send()

        @pl.when(outer >= d)
        def _(d=d):
            to_sibling(d).wait_send()


def shards(n_outer, n_inner, jacobians, weights):
    order = jacobians.shape[1]
    share = order // n_inner
    levels = log2(n_inner)
    square = (order, order)
    f32 = jnp.float32
    dma = pltpu.SemaphoreType.DMA
    return pl.pallas_call(
        functools.partial(kernel, n_outer, n_inner),
        out_shape=(jax.ShapeDtypeStruct((1,) + square, f32), jax.ShapeDtypeStruct((1, share, order), f32)),
        in_specs=[pl.BlockSpec(memory_space=pl.ANY)] * 2,
        out_specs=[pl.BlockSpec(memory_space=pltpu.VMEM)] * 2,
        scratch_shapes=[
            pltpu.VMEM((levels + 1,) + square, f32),
            pltpu.VMEM((levels,) + square, f32),
            pltpu.VMEM(square, f32),
            pltpu.VMEM(square, f32),
            pltpu.VMEM(square, f32),
            pltpu.VMEM((n_inner // 2, order // n_inner, order), f32),
            pltpu.VMEM((order // 2, order), f32),
            pltpu.VMEM(square, f32),
            pltpu.VMEM((n_outer,) + square, f32),
            pltpu.VMEM(square, f32),
            dma((2,)),
            dma((levels,)),
            dma((levels,)),
            dma((levels,)),
            dma((levels,)),
            dma((n_inner // 2,)),
            dma((n_inner // 2,)),
            dma((n_inner // 2,)),
            dma((n_inner // 2,)),
            dma((n_inner // 2,)),
            dma((n_inner // 2,)),
            dma((n_outer,)),
            dma((n_outer,)),
            dma((n_outer,)),
            dma((n_outer,)),
        ],
        compiler_params=pltpu.CompilerParams(
            collective_id=0, has_side_effects=True, vmem_limit_bytes=56 * 1024 * 1024),
    )(jacobians, weights)


def solution(mesh):
    return jax.shard_map(
        functools.partial(shards, mesh.shape["outer"], mesh.shape["inner"]),
        mesh=mesh,
        in_specs=(P(("outer", "inner"), None, None), P(("outer", "inner"), None, None)),
        out_specs=(P(("outer", "inner"), None, None), P("outer", "inner", None)),
        check_vma=False,
    )
```

```python
import functools

import jax
import jax.numpy as jnp
from jax import lax
from jax.experimental import pallas as pl
from jax.experimental.pallas import tpu as pltpu
from jax.sharding import PartitionSpec as P

MESH = pl.DeviceIdType.MESH


def split(x):
    high = x.astype(jnp.bfloat16)
    return high, (x - high.astype(jnp.float32)).astype(jnp.bfloat16)


def product(left, right, dims=((1,), (0,))):
    dot = functools.partial(
        lax.dot_general, dimension_numbers=(dims, ((), ())), preferred_element_type=jnp.float32
    )
    return dot(left[0], right[0]) + (dot(left[0], right[1]) + dot(left[1], right[0]))


def log2(n):
    return n.bit_length() - 1


def kernel(n_outer, n_inner, jac_hbm, weight_hbm, trans_ref, gram_ref,
           total, other, prefix, weight, term, terms, joined, inside, reduced, summed, starts, start,
           load_sem, send_sem, recv_sem, pass_send, pass_recv, term_send, term_recv, sum_send, sum_recv,
           sum_pass_send, sum_pass_recv,
           start_send, start_recv, start_pass_send, start_pass_recv):
    outer, inner = lax.axis_index("outer"), lax.axis_index("inner")
    order = prefix.shape[0]
    half = order // 2
    core = lax.rem(inner, 2)
    sibling = inner + 1 - 2 * core
    load_jac = pltpu.make_async_copy(jac_hbm.at[0], total.at[0], load_sem.at[0])
    load_weight = pltpu.make_async_copy(weight_hbm.at[0], weight, load_sem.at[1])
    load_jac.start()
    load_weight.start()

    def partner(index, bit):
        side = lax.rem(index // (1 << bit), 2)
        return side, index + (1 - 2 * side) * (1 << bit)

    steps = [("inner", b) for b in range(1, log2(n_inner))]
    barrier = pltpu.get_barrier_semaphore()
    pl.semaphore_signal(barrier, inc=1, device_id={"inner": sibling}, device_id_type=MESH)
    for d in range(1, n_inner // 2):
        pl.semaphore_signal(barrier, inc=1, device_id={"inner": lax.rem(inner + 2 * d, n_inner)}, device_id_type=MESH)
    for d in range(1, n_outer):
        pl.semaphore_signal(barrier, inc=1, device_id={"outer": lax.rem(outer + d, n_outer)}, device_id_type=MESH)
    pl.semaphore_wait(barrier, n_inner // 2 + n_outer - 1)

    load_jac.wait()
    swap = pltpu.make_async_remote_copy(
        total.at[0], other.at[0], pass_send.at[0], pass_recv.at[0], {"inner": sibling}, MESH)
    swap.start()
    prefix[...] = total[0]
    swap.wait()

    mine = pl.ds(pl.multiple_of(core * half, half), half)
    theirs = pl.ds(pl.multiple_of((1 - core) * half, half), half)
    share = order // n_inner

    def to_segment(d):
        return pltpu.make_async_remote_copy(
            total.at[len(steps) + 1, mine], starts.at[d, mine], start_send.at[d], start_recv.at[d],
            {"outer": lax.rem(outer + d, n_outer)}, MESH)

    def to_sibling(d):
        return pltpu.make_async_remote_copy(
            starts.at[d, mine], starts.at[d, mine], start_pass_send.at[d], start_pass_recv.at[d],
            {"inner": sibling}, MESH)

    chips = n_inner // 2
    piece = half // chips
    own = pl.ds(pl.multiple_of(inner * share, share), share)

    def rows_of(chip):
        return pl.ds(pl.multiple_of(core * half + chip * piece, piece), piece)

    def chip_at(d):
        return lax.rem(inner // 2 + d, chips)

    def to_owner(d):
        return pltpu.make_async_remote_copy(
            reduced.at[rows_of(chip_at(d))], terms.at[d], term_send.at[d], term_recv.at[d],
            {"inner": chip_at(d) * 2 + core}, MESH)

    kept = rows_of(chip_at(0))

    def to_all(d):
        return pltpu.make_async_remote_copy(
            summed.at[kept], summed.at[kept], sum_send.at[d], sum_recv.at[d],
            {"inner": chip_at(d) * 2 + core}, MESH)

    def sum_to_sibling(d):
        rows = rows_of(chip_at(chips - d))
        return pltpu.make_async_remote_copy(
            summed.at[rows], summed.at[rows], sum_pass_send.at[d], sum_pass_recv.at[d],
            {"inner": sibling}, MESH)

    sides = [core] + [partner(inner, b)[0] for _, b in steps]
    targets = [{axis: partner(inner, b)[1]} for axis, b in steps]
    join = pltpu.make_async_remote_copy(
        term, joined, term_send.at[0], term_recv.at[0], {"inner": sibling}, MESH)
    row = lax.broadcasted_iota(jnp.int32, (order, order), 0)
    inside[...] = (row == lax.broadcasted_iota(jnp.int32, (order, order), 1)).astype(jnp.float32)
    left_columns = pl.ds(pl.multiple_of(core * half, half), half)
    right_columns = pl.ds(pl.multiple_of((1 - core) * half, half), half)

    def hop(source, target, s, by_row, device, send, recv):
        part = (s, mine) if by_row else (s, slice(None), left_columns)
        return pltpu.make_async_remote_copy(
            source.at[part], target.at[part], send.at[s], recv.at[s], device, MESH)

    def on_kind(kind, act):
        @pl.when(kind == 0)
        def _():
            act(True)

        @pl.when(kind == 1)
        def _():
            act(False)

    def send_half(s, kind):
        on_kind(kind, lambda by_row: hop(total, other, s, by_row, targets[s - 1], send_sem, recv_sem).start())

    def pass_half(s, kind):
        def act(by_row):
            hop(total, other, s, by_row, targets[s - 1], send_sem, recv_sem).wait_recv()
            hop(other, other, s, by_row, {"inner": sibling}, pass_send, pass_recv).start()
        on_kind(kind, act)

    def wait_pass(s, kind):
        on_kind(kind, lambda by_row: hop(
            other, other, s, by_row, {"inner": sibling}, pass_send, pass_recv).wait_recv())

    def join_rows(s, side, rows):
        @pl.when(side == 1)
        def _():
            total[s + 1, rows] = product(split(total[s, rows]), split(other[s]))

        @pl.when(side == 0)
        def _():
            total[s + 1, rows] = product(split(other[s, rows]), split(total[s]))

    def join_early(side, mine, columns):
        @pl.when(side == 1)
        def _():
            total[2, :, columns] = product(split(total[1]), split(other[1, :, columns]))

        @pl.when(side == 0)
        def _():
            total[2, mine] = product(split(other[1, mine]), split(total[1]))

    kinds = [None, sides[1] if len(sides) > 1 else None]
    for s in range(2, len(sides)):
        kinds.append(sides[1] * 1 if s == 2 else inner * 0)
    def sent(s):
        return 1 - kinds[s] if s == 1 else kinds[s]

    for s in range(len(steps) + 1):
        side, last = sides[s], s == len(steps)
        early = s == 1 and not last
        if early:
            join_early(side, mine, left_columns)
        elif s == 0 and not last:
            join_rows(s, side, mine)
            join_rows(s, side, theirs)
        else:
            join_rows(s, side, mine)

        if last:
            for d in range(1, n_outer):
                @pl.when(outer + d < n_outer)
                def _(d=d):
                    to_segment(d).start()
        else:
            send_half(s + 1, sent(s + 1))

        if early:
            wait_pass(s, kinds[s])
            join_early(side, theirs, right_columns)
        elif not last and s > 0:
            join_rows(s, side, theirs)

        gathered = prefix if s == 0 else inside

        @pl.when(side == 1)
        def _():
            gathered[...] = product(split(gathered[...]), split(other[s]))

        if s == 0:
            current = split(prefix[...])
            load_weight.wait()
            term[...] = product(current, split(product(split(weight[...]), current)), ((0,), (0,)))
            join.start()

        if not last:
            pass_half(s + 1, kinds[s + 1])
            if s + 1 != 1 or s + 1 == len(steps):
                wait_pass(s + 1, kinds[s + 1])

    join.wait_recv()
    current = split(inside[...])
    reduced[...] = product(current, split(product(split(term[...] + joined[...]), current)), ((0,), (0,)))
    owners = [to_owner(d) for d in range(1, chips)]
    for copy in owners:
        copy.start()
    result = reduced[kept]
    for d in range(1, chips):
        owners[d - 1].wait_recv()
        result = result + terms[d]
    summed[kept] = result
    everyone = [to_all(d) for d in range(1, chips)]
    for copy in everyone:
        copy.start()
    onward = [sum_to_sibling(d) for d in range(chips)]
    onward[0].start()
    for d in range(1, n_outer):
        @pl.when(outer >= d)
        def _(d=d):
            to_segment(d).wait_recv()
            to_sibling(d).start()
    for d in range(1, chips):
        everyone[d - 1].wait_recv()
        onward[d].start()

    for d in range(1, n_outer):
        @pl.when(outer >= d)
        def _(d=d):
            to_sibling(d).wait_recv()
            if d == 1:
                start[...] = starts[d]
            else:
                start[...] = product(split(start[...]), split(starts[d]))

    @pl.when(outer == 0)
    def _():
        trans_ref[0] = product(split(prefix[...]), split(inside[...]))

    @pl.when(outer > 0)
    def _():
        before = product(split(inside[...]), split(start[...]))
        trans_ref[0] = product(split(prefix[...]), split(before))

    for copy in onward:
        copy.wait_recv()
    for copy in owners + [join]:
        copy.wait_send()

    @pl.when(outer == 0)
    def _():
        gram_ref[0] = summed[own]

    @pl.when(outer > 0)
    def _():
        first = split(start[...])
        term[...] = product(first, split(product(split(summed[...]), first)), ((0,), (0,)))
        gram_ref[0] = term[own]

    for copy in everyone + onward:
        copy.wait_send()

    def finish(s):
        on_kind(sent(s), lambda by_row: hop(
            total, other, s, by_row, targets[s - 1], send_sem, recv_sem).wait_send())
        on_kind(kinds[s], lambda by_row: hop(
            other, other, s, by_row, {"inner": sibling}, pass_send, pass_recv).wait_send())

    for s in range(1, len(sides)):
        finish(s)
    for d in range(1, n_outer):
        @pl.when(outer + d < n_outer)
        def _(d=d):
            to_segment(d).wait_send()

        @pl.when(outer >= d)
        def _(d=d):
            to_sibling(d).wait_send()


def shards(n_outer, n_inner, jacobians, weights):
    order = jacobians.shape[1]
    share = order // n_inner
    levels = log2(n_inner)
    square = (order, order)
    f32 = jnp.float32
    dma = pltpu.SemaphoreType.DMA
    return pl.pallas_call(
        functools.partial(kernel, n_outer, n_inner),
        out_shape=(jax.ShapeDtypeStruct((1,) + square, f32), jax.ShapeDtypeStruct((1, share, order), f32)),
        in_specs=[pl.BlockSpec(memory_space=pl.ANY)] * 2,
        out_specs=[pl.BlockSpec(memory_space=pltpu.VMEM)] * 2,
        scratch_shapes=[
            pltpu.VMEM((levels + 1,) + square, f32),
            pltpu.VMEM((levels,) + square, f32),
            pltpu.VMEM(square, f32),
            pltpu.VMEM(square, f32),
            pltpu.VMEM(square, f32),
            pltpu.VMEM((n_inner // 2, order // n_inner, order), f32),
            pltpu.VMEM(square, f32),
            pltpu.VMEM(square, f32),
            pltpu.VMEM(square, f32),
            pltpu.VMEM(square, f32),
            pltpu.VMEM((n_outer,) + square, f32),
            pltpu.VMEM(square, f32),
            dma((2,)),
            dma((levels,)),
            dma((levels,)),
            dma((levels,)),
            dma((levels,)),
            dma((n_inner // 2,)),
            dma((n_inner // 2,)),
            dma((n_inner // 2,)),
            dma((n_inner // 2,)),
            dma((n_inner // 2,)),
            dma((n_inner // 2,)),
            dma((n_outer,)),
            dma((n_outer,)),
            dma((n_outer,)),
            dma((n_outer,)),
        ],
        compiler_params=pltpu.CompilerParams(
            collective_id=0, has_side_effects=True, vmem_limit_bytes=56 * 1024 * 1024),
    )(jacobians, weights)


def solution(mesh):
    return jax.shard_map(
        functools.partial(shards, mesh.shape["outer"], mesh.shape["inner"]),
        mesh=mesh,
        in_specs=(P(("outer", "inner"), None, None), P(("outer", "inner"), None, None)),
        out_specs=(P(("outer", "inner"), None, None), P("outer", "inner", None)),
        check_vma=False,
    )
```

```python
import functools

import jax
import jax.numpy as jnp
from jax import lax
from jax.experimental import pallas as pl
from jax.experimental.pallas import tpu as pltpu
from jax.sharding import PartitionSpec as P

MESH = pl.DeviceIdType.MESH


def split(x):
    high = x.astype(jnp.bfloat16)
    return high, (x - high.astype(jnp.float32)).astype(jnp.bfloat16)


def product(left, right, dims=((1,), (0,))):
    dot = functools.partial(
        lax.dot_general, dimension_numbers=(dims, ((), ())), preferred_element_type=jnp.float32
    )
    return dot(left[0], right[0]) + (dot(left[0], right[1]) + dot(left[1], right[0]))


def log2(n):
    return n.bit_length() - 1


def kernel(n_outer, n_inner, jac_hbm, weight_hbm, trans_ref, gram_ref,
           total, other, prefix, weight, term, terms, joined, inside, reduced, summed, starts, start,
           load_sem, send_sem, recv_sem, pass_send, pass_recv, term_send, term_recv, sum_send, sum_recv,
           sum_pass_send, sum_pass_recv,
           start_send, start_recv, start_pass_send, start_pass_recv):
    outer, inner = lax.axis_index("outer"), lax.axis_index("inner")
    order = prefix.shape[0]
    half = order // 2
    core = lax.rem(inner, 2)
    sibling = inner + 1 - 2 * core
    load_jac = pltpu.make_async_copy(jac_hbm.at[0], total.at[0], load_sem.at[0])
    load_weight = pltpu.make_async_copy(weight_hbm.at[0], weight, load_sem.at[1])
    load_jac.start()
    load_weight.start()

    def partner(index, bit):
        side = lax.rem(index // (1 << bit), 2)
        return side, index + (1 - 2 * side) * (1 << bit)

    steps = [("inner", b) for b in range(1, log2(n_inner))]
    barrier = pltpu.get_barrier_semaphore()
    pl.semaphore_signal(barrier, inc=1, device_id={"inner": sibling}, device_id_type=MESH)
    for d in range(1, n_inner // 2):
        pl.semaphore_signal(barrier, inc=1, device_id={"inner": lax.rem(inner + 2 * d, n_inner)}, device_id_type=MESH)
    for d in range(1, n_outer):
        pl.semaphore_signal(barrier, inc=1, device_id={"outer": lax.rem(outer + d, n_outer)}, device_id_type=MESH)
    pl.semaphore_wait(barrier, n_inner // 2 + n_outer - 1)

    load_jac.wait()
    swap = pltpu.make_async_remote_copy(
        total.at[0], other.at[0], pass_send.at[0], pass_recv.at[0], {"inner": sibling}, MESH)
    swap.start()
    prefix[...] = total[0]
    swap.wait()

    mine = pl.ds(pl.multiple_of(core * half, half), half)
    theirs = pl.ds(pl.multiple_of((1 - core) * half, half), half)
    share = order // n_inner

    def to_segment(d):
        return pltpu.make_async_remote_copy(
            total.at[len(steps) + 1, mine], starts.at[d, mine], start_send.at[d], start_recv.at[d],
            {"outer": lax.rem(outer + d, n_outer)}, MESH)

    def to_sibling(d):
        return pltpu.make_async_remote_copy(
            starts.at[d, mine], starts.at[d, mine], start_pass_send.at[d], start_pass_recv.at[d],
            {"inner": sibling}, MESH)

    chips = n_inner // 2
    piece = half // chips
    own = pl.ds(pl.multiple_of(inner * share, share), share)

    def rows_of(chip):
        return pl.ds(pl.multiple_of(core * half + chip * piece, piece), piece)

    def chip_at(d):
        return lax.rem(inner // 2 + d, chips)

    def to_owner(d):
        return pltpu.make_async_remote_copy(
            reduced.at[rows_of(chip_at(d))], terms.at[d], term_send.at[d], term_recv.at[d],
            {"inner": chip_at(d) * 2 + core}, MESH)

    kept = rows_of(chip_at(0))

    def to_all(d):
        return pltpu.make_async_remote_copy(
            summed.at[kept], summed.at[kept], sum_send.at[d], sum_recv.at[d],
            {"inner": chip_at(d) * 2 + core}, MESH)

    def sum_to_sibling(d):
        rows = rows_of(chip_at(chips - d))
        return pltpu.make_async_remote_copy(
            summed.at[rows], summed.at[rows], sum_pass_send.at[d], sum_pass_recv.at[d],
            {"inner": sibling}, MESH)

    sides = [core] + [partner(inner, b)[0] for _, b in steps]
    targets = [{axis: partner(inner, b)[1]} for axis, b in steps]
    join = pltpu.make_async_remote_copy(
        term, joined, term_send.at[0], term_recv.at[0], {"inner": sibling}, MESH)
    row = lax.broadcasted_iota(jnp.int32, (order, order), 0)
    inside[...] = (row == lax.broadcasted_iota(jnp.int32, (order, order), 1)).astype(jnp.float32)
    left_columns = pl.ds(pl.multiple_of(core * half, half), half)
    right_columns = pl.ds(pl.multiple_of((1 - core) * half, half), half)

    def hop(source, target, s, by_row, device, send, recv):
        part = (s, mine) if by_row else (s, slice(None), left_columns)
        return pltpu.make_async_remote_copy(
            source.at[part], target.at[part], send.at[s], recv.at[s], device, MESH)

    def on_kind(kind, act):
        @pl.when(kind == 0)
        def _():
            act(True)

        @pl.when(kind == 1)
        def _():
            act(False)

    def send_half(s, kind):
        on_kind(kind, lambda by_row: hop(total, other, s, by_row, targets[s - 1], send_sem, recv_sem).start())

    def pass_half(s, kind):
        def act(by_row):
            hop(total, other, s, by_row, targets[s - 1], send_sem, recv_sem).wait_recv()
            hop(other, other, s, by_row, {"inner": sibling}, pass_send, pass_recv).start()
        on_kind(kind, act)

    def wait_pass(s, kind):
        on_kind(kind, lambda by_row: hop(
            other, other, s, by_row, {"inner": sibling}, pass_send, pass_recv).wait_recv())

    def join_rows(s, side, rows):
        @pl.when(side == 1)
        def _():
            total[s + 1, rows] = product(split(total[s, rows]), split(other[s]))

        @pl.when(side == 0)
        def _():
            total[s + 1, rows] = product(split(other[s, rows]), split(total[s]))

    def join_early(side, mine, columns):
        @pl.when(side == 1)
        def _():
            total[2, :, columns] = product(split(total[1]), split(other[1, :, columns]))

        @pl.when(side == 0)
        def _():
            total[2, mine] = product(split(other[1, mine]), split(total[1]))

    kinds = [None, sides[1] if len(sides) > 1 else None]
    for s in range(2, len(sides)):
        kinds.append(sides[1] * 1 if s == 2 else inner * 0)
    def sent(s):
        return 1 - kinds[s] if s == 1 else kinds[s]

    for s in range(len(steps) + 1):
        side, last = sides[s], s == len(steps)
        early = s == 1 and not last
        if early:
            join_early(side, mine, left_columns)
        elif s == 0 and not last:
            join_rows(s, side, mine)
            join_rows(s, side, theirs)
        elif not last:
            join_rows(s, side, mine)

        if not last:
            send_half(s + 1, sent(s + 1))

        if early:
            wait_pass(s, kinds[s])
            join_early(side, theirs, right_columns)
        elif not last and s > 0:
            join_rows(s, side, theirs)

        gathered = prefix if s == 0 else inside

        @pl.when(side == 1)
        def _():
            gathered[...] = product(split(gathered[...]), split(other[s]))

        if s == 0:
            current = split(prefix[...])
            load_weight.wait()
            term[...] = product(current, split(product(split(weight[...]), current)), ((0,), (0,)))
            join.start()

        if not last:
            pass_half(s + 1, kinds[s + 1])
            if s + 1 != 1 or s + 1 == len(steps):
                wait_pass(s + 1, kinds[s + 1])

    join.wait_recv()
    current = split(inside[...])
    reduced[...] = product(current, split(product(split(term[...] + joined[...]), current)), ((0,), (0,)))
    owners = [to_owner(d) for d in range(1, chips)]
    for copy in owners:
        copy.start()
    join_rows(len(steps), sides[-1], mine)
    for d in range(1, n_outer):
        @pl.when(outer + d < n_outer)
        def _(d=d):
            to_segment(d).start()
    result = reduced[kept]
    for d in range(1, chips):
        owners[d - 1].wait_recv()
        result = result + terms[d]
    summed[kept] = result
    everyone = [to_all(d) for d in range(1, chips)]
    for copy in everyone:
        copy.start()
    onward = [sum_to_sibling(d) for d in range(chips)]
    onward[0].start()
    for d in range(1, n_outer):
        @pl.when(outer >= d)
        def _(d=d):
            to_segment(d).wait_recv()
            to_sibling(d).start()
    for d in range(1, chips):
        everyone[d - 1].wait_recv()
        onward[d].start()

    for d in range(1, n_outer):
        @pl.when(outer >= d)
        def _(d=d):
            to_sibling(d).wait_recv()
            if d == 1:
                start[...] = starts[d]
            else:
                start[...] = product(split(start[...]), split(starts[d]))

    @pl.when(outer == 0)
    def _():
        trans_ref[0] = product(split(prefix[...]), split(inside[...]))

    @pl.when(outer > 0)
    def _():
        before = product(split(inside[...]), split(start[...]))
        trans_ref[0] = product(split(prefix[...]), split(before))

    for copy in onward:
        copy.wait_recv()
    for copy in owners + [join]:
        copy.wait_send()

    @pl.when(outer == 0)
    def _():
        gram_ref[0] = summed[own]

    @pl.when(outer > 0)
    def _():
        first = split(start[...])
        term[...] = product(first, split(product(split(summed[...]), first)), ((0,), (0,)))
        gram_ref[0] = term[own]

    for copy in everyone + onward:
        copy.wait_send()

    def finish(s):
        on_kind(sent(s), lambda by_row: hop(
            total, other, s, by_row, targets[s - 1], send_sem, recv_sem).wait_send())
        on_kind(kinds[s], lambda by_row: hop(
            other, other, s, by_row, {"inner": sibling}, pass_send, pass_recv).wait_send())

    for s in range(1, len(sides)):
        finish(s)
    for d in range(1, n_outer):
        @pl.when(outer + d < n_outer)
        def _(d=d):
            to_segment(d).wait_send()

        @pl.when(outer >= d)
        def _(d=d):
            to_sibling(d).wait_send()


def shards(n_outer, n_inner, jacobians, weights):
    order = jacobians.shape[1]
    share = order // n_inner
    levels = log2(n_inner)
    square = (order, order)
    f32 = jnp.float32
    dma = pltpu.SemaphoreType.DMA
    return pl.pallas_call(
        functools.partial(kernel, n_outer, n_inner),
        out_shape=(jax.ShapeDtypeStruct((1,) + square, f32), jax.ShapeDtypeStruct((1, share, order), f32)),
        in_specs=[pl.BlockSpec(memory_space=pl.ANY)] * 2,
        out_specs=[pl.BlockSpec(memory_space=pltpu.VMEM)] * 2,
        scratch_shapes=[
            pltpu.VMEM((levels + 1,) + square, f32),
            pltpu.VMEM((levels,) + square, f32),
            pltpu.VMEM(square, f32),
            pltpu.VMEM(square, f32),
            pltpu.VMEM(square, f32),
            pltpu.VMEM((n_inner // 2, order // n_inner, order), f32),
            pltpu.VMEM(square, f32),
            pltpu.VMEM(square, f32),
            pltpu.VMEM(square, f32),
            pltpu.VMEM(square, f32),
            pltpu.VMEM((n_outer,) + square, f32),
            pltpu.VMEM(square, f32),
            dma((2,)),
            dma((levels,)),
            dma((levels,)),
            dma((levels,)),
            dma((levels,)),
            dma((n_inner // 2,)),
            dma((n_inner // 2,)),
            dma((n_inner // 2,)),
            dma((n_inner // 2,)),
            dma((n_inner // 2,)),
            dma((n_inner // 2,)),
            dma((n_outer,)),
            dma((n_outer,)),
            dma((n_outer,)),
            dma((n_outer,)),
        ],
        compiler_params=pltpu.CompilerParams(
            collective_id=0, has_side_effects=True, vmem_limit_bytes=56 * 1024 * 1024),
    )(jacobians, weights)


def solution(mesh):
    return jax.shard_map(
        functools.partial(shards, mesh.shape["outer"], mesh.shape["inner"]),
        mesh=mesh,
        in_specs=(P(("outer", "inner"), None, None), P(("outer", "inner"), None, None)),
        out_specs=(P(("outer", "inner"), None, None), P("outer", "inner", None)),
        check_vma=False,
    )
```
